768 devices in a mesh: row: 32 (over z_hi, x, core), col: 24 (over z_lo, y).
Axes of the slice: x: 4, y: 8, z: 12 (z_hi: 4, z_lo: 3; z = z_hi * 3 + z_lo), core: 2. Of those that a mesh axis runs over, the one named last changes fastest.
Arguments:
- img_raw: bfloat16 [18432, 1152], P(('row', 'col')), may hold values from -0.1875 to 0.1875
- txt_raw: bfloat16 [18432, 1152], P(('col', 'row')), may hold values from -0.1875 to 0.1875
- labels: int32 [18432], P(('row', 'col')), may hold values from 0 to 18431, each once
- log_logit_scale: float32 [1], replicated, may hold values from 1 to 1.6
- bias: float32 [1], replicated, may hold values from -3 to -1.5
Outputs:
- img_grad: float32 [18432, 1152], P(('row', 'col'))
- txt_grad: float32 [18432, 1152], P(('col', 'row'))
The draws below stay inside these ranges and needn't reach their ends.
Inputs may be any that keep to these rules, and one draw needn't show every extreme that they name: labels is a permutation: every text is the positive of exactly one image.
All inputs are finite; a program needn't handle non-finite values.
Results may differ from the reference program's by a relative error of at most 0.0043.
Values may be sent and summed in bfloat16 or wider, within the bound.
No kernel may reach another device: no remote copies, remote signals or barrier semaphores. Data moves between devices by JAX's collectives and lax.ppermute only.
A program may use at most 32 MiB of HBM per device.

```python
import jax
import jax.numpy as jnp
from jax import lax

D = 1152
BLK = 24
BATCH = 18432
N_ROW = 32
N_COL = 24


def block_levels(rng, extent, split, least, top_value):
    def one(position, blocks):
        draws = jax.random.uniform(jax.random.fold_in(jax.random.fold_in(rng, 6), position), (blocks,), jnp.float32, least / len(split), top_value / len(split))
        return jnp.repeat(jnp.exp(draws), extent[position] // blocks).reshape((-1,) + (1,) * (len(extent) - position - 1))

    factor_of = one(*split[0])
    for cut in split[1:]:
        factor_of = factor_of * one(*cut)
    return factor_of


def noise(rng, dims, deviation, limit, split=(), held_as=jnp.bfloat16):
    result = jax.random.normal(rng, dims, jnp.float32) * deviation
    if len(split) > 0:
        result = block_levels(rng, dims, split, -0.22, 0.18) * result
    return jnp.clip(result, min=-limit, max=limit).astype(held_as)


def setup_inputs(seed: int = 0) -> dict:
    seeds = jax.random.split(jax.random.key(seed), 6)
    img_raw = noise(seeds[0], (BATCH, D), D ** -0.5, 0.1875, ((0, 768),))
    txt_raw = noise(seeds[1], (BATCH, D), D ** -0.5, 0.1875, ((0, 768),))
    labels = jax.random.permutation(seeds[2], BATCH).astype(jnp.int32)
    log_logit_scale = jnp.clip(jax.random.uniform(seeds[3], (1,), jnp.float32, 1.0, 1.6), 1.0, 1.6)
    bias = jnp.clip(jax.random.uniform(seeds[4], (1,), jnp.float32, -3.0, -1.5), -3.0, -1.5)
    return dict(img_raw=img_raw, txt_raw=txt_raw, labels=labels, log_logit_scale=log_logit_scale, bias=bias)


EPS = 1e-06

def normalize(raw):
    wide = raw.astype(jnp.float32)
    inverse = lax.rsqrt(lax.optimization_barrier(jnp.sum(wide * wide, axis=-1, keepdims=True)) + EPS)
    return (wide * inverse, inverse)

def project_back(hat, inverse, dnorm):
    return (dnorm - hat * lax.optimization_barrier(jnp.sum(hat * dnorm, axis=-1, keepdims=True))) * inverse

def reference(img_raw, txt_raw, labels, log_logit_scale, bias):
    logit_scaling = jnp.exp(log_logit_scale[0])
    block_shift = bias[0]
    img_hat, img_inv = normalize(img_raw)
    txt_hat, txt_inv = normalize(txt_raw)
    img_norm = img_hat.astype(jnp.bfloat16)
    caption_norm = txt_hat.astype(jnp.bfloat16)
    total = img_raw.shape[0]
    columns = jnp.arange(total, dtype=jnp.int32)
    img_blocks = img_norm.reshape(N_ROW, BLK * N_COL, img_norm.shape[1])
    label_blocks = labels.reshape(N_ROW, BLK * N_COL)

    def step(loop_accumulator, block):
        rows, lab = block
        pair_logits = lax.dot_general(rows, caption_norm, (((1,), (1,)), ((), ())), preferred_element_type=jnp.float32)
        matching_pair_mask = (lab[:, None] == columns[None, :]).astype(jnp.float32)
        gradient_block = (jax.nn.sigmoid(logit_scaling * pair_logits + block_shift) - matching_pair_mask).astype(jnp.bfloat16)
        picture_portion = logit_scaling * jnp.dot(gradient_block, caption_norm, preferred_element_type=jnp.float32)
        caption_portion = lax.dot_general(gradient_block, rows, (((0,), (0,)), ((), ())), preferred_element_type=jnp.float32)
        return (loop_accumulator + logit_scaling * caption_portion, picture_portion)
    txt_dnorm, img_parts = lax.scan(step, jnp.zeros(caption_norm.shape, jnp.float32), (img_blocks, label_blocks))
    img_dnorm = img_parts.reshape(total, img_norm.shape[1])
    img_grad = project_back(img_hat, img_inv, img_dnorm)
    txt_grad = project_back(txt_hat, txt_inv, txt_dnorm)
    return (img_grad, txt_grad)
```

```python
import jax
import jax.numpy as jnp
from jax import lax
from jax.sharding import Mesh, PartitionSpec as P

EPS = 1e-06
BF = jnp.bfloat16
F32 = jnp.float32
SWAP = [(0, 1), (1, 0)]


def normalize(raw):
    wide = raw.astype(F32)
    inverse = lax.rsqrt(jnp.sum(wide * wide, axis=-1, keepdims=True) + EPS)
    return (wide * inverse, inverse)


def project_back(hat, inverse, dnorm):
    return (dnorm - hat * jnp.sum(hat * dnorm, axis=-1, keepdims=True)) * inverse


def exchange(blocks, axes):
    return lax.all_to_all(blocks, axes, split_axis=0, concat_axis=0, tiled=True)


def spread(block, axes, count):
    return exchange(jnp.broadcast_to(block[None], (count,) + block.shape), axes)


def on_device(img_raw, txt_raw, labels, log_logit_scale, bias):
    blk, width = img_raw.shape
    n_zh, n_x, n_zl, n_y = (lax.axis_size(a) for a in ("zh", "x", "zl", "y"))
    temperature = jnp.exp(log_logit_scale[0])
    shift = bias[0]
    img_hat, img_inv = normalize(img_raw)
    txt_hat, txt_inv = normalize(txt_raw)

    high = labels // 256
    tail = jnp.stack([high, labels - 256 * high], axis=1).astype(BF)
    tail = jnp.pad(tail, ((0, 0), (0, 126)))
    packed = jnp.concatenate([img_hat.astype(BF), tail], axis=1)
    packed = spread(packed, "zl", n_zl)
    packed, txt_block = lax.optimization_barrier((packed, txt_hat.astype(BF)))
    packed = lax.all_gather(packed.reshape(n_zl * blk, -1), "y", axis=0, tiled=True)
    txt_own = spread(txt_block, ("zh", "x"), n_zh * n_x).reshape(n_zh * n_x * blk, width)
    txt_far = lax.ppermute(txt_own, "c", SWAP)

    img = packed[:, :width]
    marks = packed[:, width : width + 2].astype(F32)
    target = (marks[:, :1] * 256.0 + marks[:, 1:]).astype(jnp.int32)

    column_block = (lax.axis_index("zl") * n_y + lax.axis_index("y")) * (n_zh * n_x * 2)
    core = lax.axis_index("c")
    place = jnp.arange(n_zh * n_x * blk, dtype=jnp.int32)

    def pair_grad(txt, half):
        scores = lax.dot_general(img, txt, (((1,), (1,)), ((), ())), preferred_element_type=F32)
        columns = (column_block + (place // blk) * 2 + half) * blk + place % blk
        positive = (target == columns[None, :]).astype(F32)
        return (jax.nn.sigmoid(temperature * scores + shift) - positive).astype(BF)

    grad_own = pair_grad(txt_own, core)
    grad_far = pair_grad(txt_far, 1 - core)

    def txt_part(grad):
        return temperature * lax.dot_general(
            grad, img, (((0,), (0,)), ((), ())), preferred_element_type=F32
        )

    arrived = lax.ppermute(txt_part(grad_far).astype(BF), "c", SWAP)
    txt_sum = txt_part(grad_own) + arrived.astype(F32)
    txt_blocks = exchange(txt_sum.astype(BF).reshape(n_zh * n_x, blk, width), ("zh", "x"))
    txt_dnorm = jnp.sum(txt_blocks.astype(F32), axis=0)

    img_sum = temperature * (
        jnp.dot(grad_own, txt_own, preferred_element_type=F32)
        + jnp.dot(grad_far, txt_far, preferred_element_type=F32)
    )
    img_blocks = exchange(img_sum.astype(BF).reshape(n_y * n_zl, blk, width), ("y", "zl"))
    img_dnorm = jnp.sum(img_blocks.astype(F32), axis=0)

    return (project_back(img_hat, img_inv, img_dnorm), project_back(txt_hat, txt_inv, txt_dnorm))


def solution(mesh):
    fine = Mesh(mesh.devices.reshape(4, 4, 2, 3, 8), ("zh", "x", "c", "zl", "y"))
    row, col = ("zh", "x", "c"), ("zl", "y")
    return jax.shard_map(
        on_device,
        mesh=fine,
        in_specs=(P(row + col, None), P(col + row, None), P(row + col), P(), P()),
        out_specs=(P(row + col, None), P(col + row, None)),
        check_vma=False,
    )
```

```python
import jax
import jax.numpy as jnp
from jax import lax
from jax.sharding import Mesh, PartitionSpec as P

EPS = 1e-06
BF = jnp.bfloat16
F32 = jnp.float32
STEPS = (("zh", 2), ("zh", 1), ("x", 2), ("x", 1), ("c", 1))


def normalize(raw):
    wide = raw.astype(F32)
    inverse = lax.rsqrt(jnp.sum(wide * wide, axis=-1, keepdims=True) + EPS)
    return (wide * inverse, inverse)


def project_back(hat, inverse, dnorm):
    return (dnorm - hat * jnp.sum(hat * dnorm, axis=-1, keepdims=True)) * inverse


def exchange(blocks, axes):
    return lax.all_to_all(blocks, axes, split_axis=0, concat_axis=0, tiled=True)


def spread(block, axis):
    count = lax.axis_size(axis)
    copies = jnp.broadcast_to(block[None], (count,) + block.shape)
    return exchange(copies, axis).reshape(count * block.shape[0], block.shape[1])


def gather_sum(part, axis):
    count = lax.axis_size(axis)
    blocks = part.astype(BF).reshape(count, part.shape[0] // count, part.shape[1])
    return jnp.sum(exchange(blocks, axis).astype(F32), axis=0)


def partner(x, axis, bit):
    return lax.ppermute(x, axis, [(i, i ^ bit) for i in range(lax.axis_size(axis))])


def on_device(img_raw, txt_raw, labels, log_logit_scale, bias):
    blk, width = img_raw.shape
    n_x, n_c, n_zl, n_y = (lax.axis_size(a) for a in ("x", "c", "zl", "y"))
    temperature = jnp.exp(log_logit_scale[0])
    shift = bias[0]
    img_hat, img_inv = normalize(img_raw)
    txt_hat, txt_inv = normalize(txt_raw)

    high = labels // 256
    tail = jnp.stack([high, labels - 256 * high], axis=1).astype(BF)
    tail = jnp.pad(tail, ((0, 0), (0, 126)))
    packed = jnp.concatenate([img_hat.astype(BF), tail], axis=1)
    packed = spread(packed, "zl")

    txt = txt_hat.astype(BF)
    owner = jnp.zeros((1,), jnp.int32)
    for step, (axis, bit) in enumerate(STEPS):
        weight = bit * {"zh": n_x * n_c, "x": n_c, "c": 1}[axis]
        txt = jnp.concatenate([txt, partner(txt, axis, bit)], axis=0)
        owner = jnp.concatenate([owner, owner ^ weight])
        if step == 0:
            txt, packed = lax.optimization_barrier((txt, packed))
            packed = spread(packed, "y")
    n_row = owner.shape[0]
    half = n_row // 2 * blk

    img = packed[:, :width]
    marks = packed[:, width : width + 2].astype(F32)
    target = (marks[:, :1] * 256.0 + marks[:, 1:]).astype(jnp.int32)

    me = (lax.axis_index("zh") * n_x + lax.axis_index("x")) * n_c + lax.axis_index("c")
    first = (lax.axis_index("zl") * n_y + lax.axis_index("y")) * n_row
    columns = (first + (owner ^ me))[:, None] * blk + jnp.arange(blk, dtype=jnp.int32)[None, :]
    scores = lax.dot_general(img, txt, (((1,), (1,)), ((), ())), preferred_element_type=F32)
    positive = (target == columns.reshape(1, -1)).astype(F32)
    grad = (jax.nn.sigmoid(temperature * scores + shift) - positive).astype(BF)

    def txt_part(part):
        return lax.dot_general(part, img, (((0,), (0,)), ((), ())), preferred_element_type=F32)

    arrived = partner(txt_part(grad[:, half:]).astype(BF), *STEPS[-1])
    txt_sum = txt_part(grad[:, :half]) + arrived.astype(F32)
    for axis, bit in STEPS[-2::-1]:
        half = txt_sum.shape[0] // 2
        arrived = partner(txt_sum[half:].astype(BF), axis, bit)
        txt_sum = txt_sum[:half] + arrived.astype(F32)

    img_sum = jnp.dot(grad, txt, preferred_element_type=F32)
    img_sum = gather_sum(gather_sum(img_sum, "y"), "zl")

    return (
        project_back(img_hat, img_inv, temperature * img_sum),
        project_back(txt_hat, txt_inv, temperature * txt_sum),
    )


def solution(mesh):
    fine = Mesh(mesh.devices.reshape(4, 4, 2, 3, 8), ("zh", "x", "c", "zl", "y"))
    row, col = ("zh", "x", "c"), ("zl", "y")
    return jax.shard_map(
        on_device,
        mesh=fine,
        in_specs=(P(row + col, None), P(col + row, None), P(row + col), P(), P()),
        out_specs=(P(row + col, None), P(col + row, None)),
        check_vma=False,
    )
```

```python
import jax
import jax.numpy as jnp
from jax import lax
from jax.experimental import pallas as pl
from jax.experimental.pallas import tpu as pltpu
from jax.sharding import Mesh, PartitionSpec as P

EPS = 1e-06
BF = jnp.bfloat16
F32 = jnp.float32
Z = ("zh", "zl")
RUN = 4


def normalize(raw):
    wide = raw.astype(F32)
    inverse = lax.rsqrt(jnp.sum(wide * wide, axis=-1, keepdims=True) + EPS)
    return (wide * inverse, inverse)


def prepare(img_ref, txt_ref, label_ref, packed_ref, copies_ref, img_inv_ref, txt_inv_ref):
    blk, width = img_ref.shape
    img_hat, img_inv_ref[...] = normalize(img_ref[...])
    packed_ref[:, :width] = img_hat.astype(BF)
    row = lax.broadcasted_iota(jnp.int32, (blk, blk), 0)
    lane = lax.broadcasted_iota(jnp.int32, (blk, blk), 1)
    spot = jnp.where(row == lane, label_ref[...].astype(F32), 0.0)
    label = jnp.sum(spot, axis=1, keepdims=True).astype(jnp.int32)
    high = label >> 8
    place = lax.broadcasted_iota(jnp.int32, (blk, packed_ref.shape[1] - width), 1)
    tail = jnp.where(place == 0, high, jnp.where(place == 1, label - 256 * high, 0))
    packed_ref[:, width:] = tail.astype(F32).astype(BF)
    txt_hat, txt_inv_ref[...] = normalize(txt_ref[...])
    txt = txt_hat.astype(BF)
    for i in range(copies_ref.shape[0]):
        copies_ref[i] = txt


def project_back(raw, inverse, dnorm):
    hat = raw.astype(F32) * inverse
    return (dnorm - hat * jnp.sum(hat * dnorm, axis=-1, keepdims=True)) * inverse


def exchange(blocks, axes):
    groups = None
    if axes == Z:
        groups = [list(range(i, i + RUN)) for i in range(0, lax.axis_size(Z), RUN)]
    return lax.all_to_all(
        blocks, axes, split_axis=0, concat_axis=0, axis_index_groups=groups, tiled=True
    )


def spread(block, axes, count):
    copies = jnp.broadcast_to(block[None], (count,) + block.shape)
    return joined(exchange(copies, axes))


def joined(blocks):
    return blocks.reshape(-1, blocks.shape[-1])


def scattered(part, axes, count):
    blocks = part.astype(BF).reshape(count, part.shape[0] // count, part.shape[1])
    return exchange(blocks, axes)


def send(x, axis, hop):
    size = lax.axis_size(axis)
    return lax.ppermute(x.astype(BF), axis, [(i, (i + hop) % size) for i in range(size)])


def on_device(img_raw, txt_raw, labels, log_logit_scale, bias):
    blk, width = img_raw.shape
    n_z, n_zl, n_x, n_c, n_y = (lax.axis_size(a) for a in (Z, "zl", "x", "c", "y"))
    temperature = jnp.exp(log_logit_scale[0])
    shift = bias[0]
    vmem = pl.BlockSpec(memory_space=pltpu.VMEM)
    packed, txt, img_inv, txt_inv = pl.pallas_call(
        prepare,
        out_shape=[
            jax.ShapeDtypeStruct((blk, width + 128), BF),
            jax.ShapeDtypeStruct((RUN, blk, width), BF),
            jax.ShapeDtypeStruct((blk, 1), F32),
            jax.ShapeDtypeStruct((blk, 1), F32),
        ],
        in_specs=[vmem] * 3,
        out_specs=[vmem] * 4,
    )(img_raw, txt_raw, labels.reshape(1, blk))

    trio = jnp.concatenate([packed, send(packed, Z, -RUN), send(packed, Z, RUN)])
    trio, txt = lax.optimization_barrier((trio, joined(exchange(txt, Z))))
    wide = jnp.concatenate([send(trio, "y", 3), trio, send(trio, "y", -3)])
    y = trio.shape[0]
    packed = jnp.concatenate([wide, send(wide, "y", -1), send(wide[y:], "y", 1)])
    txt = spread(txt, "x", n_x)
    half = txt.shape[0]
    txt = jnp.concatenate([txt, send(txt, "c", 1)])

    img = packed[:, :width]
    marks = packed[:, width : width + 2].astype(F32)
    target = (marks[:, :1] * 256.0 + marks[:, 1:]).astype(jnp.int32)

    owner = jnp.arange(n_c * n_x * RUN, dtype=jnp.int32)
    at_z = lax.axis_index(Z) // RUN * RUN + owner % RUN
    at_x = owner // RUN % n_x
    at_c = (lax.axis_index("c") + owner // (RUN * n_x)) % n_c
    col = at_z % n_zl * n_y + lax.axis_index("y")
    block = ((col * (n_z // n_zl) + at_z // n_zl) * n_x + at_x) * n_c + at_c
    columns = block[:, None] * blk + jnp.arange(blk, dtype=jnp.int32)[None, :]
    scores = lax.dot_general(img, txt, (((1,), (1,)), ((), ())), preferred_element_type=F32)
    positive = (target == columns.reshape(1, -1)).astype(F32)
    grad = (jax.nn.sigmoid(temperature * scores + shift) - positive).astype(BF)

    def txt_part(part):
        return lax.dot_general(part, img, (((0,), (0,)), ((), ())), preferred_element_type=F32)

    away = jnp.dot(grad[3 * y :], txt, preferred_element_type=F32).astype(BF)
    away, grad = lax.optimization_barrier((away, grad))
    before, after = send(away[: 3 * y], "y", 1), send(away[3 * y :], "y", -1)

    arrived = send(txt_part(grad[:, half:]), "c", 1)
    txt_sum = txt_part(grad[:, :half]) + arrived.astype(F32)
    txt_sum = jnp.sum(scattered(txt_sum, "x", n_x).astype(F32), axis=0)
    txt_sum = jnp.sum(scattered(txt_sum, Z, RUN).astype(F32), axis=0)

    mine = jnp.dot(grad[: 3 * y], txt, preferred_element_type=F32)
    low = mine[:y] + before[:y].astype(F32)
    mid = mine[y : 2 * y] + before[y : 2 * y].astype(F32) + after[:y].astype(F32)
    top = mine[2 * y :] + before[2 * y :].astype(F32) + after[y:].astype(F32)
    mid = mid + send(low, "y", -3).astype(F32) + send(top, "y", 3).astype(F32)
    one, two = send(mid[blk : 2 * blk], Z, RUN), send(mid[2 * blk :], Z, -RUN)
    img_sum = mid[:blk] + one.astype(F32) + two.astype(F32)
    return (
        project_back(img_raw, img_inv, temperature * img_sum),
        project_back(txt_raw, txt_inv, temperature * txt_sum),
    )


def solution(mesh):
    fine = Mesh(mesh.devices.reshape(4, 4, 2, 3, 8), ("zh", "x", "c", "zl", "y"))
    row, col = ("zh", "x", "c"), ("zl", "y")
    return jax.shard_map(
        on_device,
        mesh=fine,
        in_specs=(P(row + col, None), P(col + row, None), P(row + col), P(), P()),
        out_specs=(P(row + col, None), P(col + row, None)),
        check_vma=False,
    )
```

```python
import jax
import jax.numpy as jnp
from jax import lax
from jax.experimental import pallas as pl
from jax.experimental.pallas import tpu as pltpu
from jax.sharding import Mesh, PartitionSpec as P

EPS = 1e-06
BF = jnp.bfloat16
F32 = jnp.float32
Z = ("zh", "zl")
RUN = 4


def normalize(raw):
    wide = raw.astype(F32)
    inverse = lax.rsqrt(jnp.sum(wide * wide, axis=-1, keepdims=True) + EPS)
    return (wide * inverse, inverse)


def prepare(img_ref, txt_ref, label_ref, packed_ref, copies_ref, img_inv_ref, txt_inv_ref):
    blk, width = img_ref.shape
    img_hat, img_inv_ref[...] = normalize(img_ref[...])
    packed_ref[:, :width] = img_hat.astype(BF)
    row = lax.broadcasted_iota(jnp.int32, (blk, blk), 0)
    lane = lax.broadcasted_iota(jnp.int32, (blk, blk), 1)
    spot = jnp.where(row == lane, label_ref[...].astype(F32), 0.0)
    label = jnp.sum(spot, axis=1, keepdims=True).astype(jnp.int32)
    high = label >> 8
    place = lax.broadcasted_iota(jnp.int32, (blk, packed_ref.shape[1] - width), 1)
    tail = jnp.where(place == 0, high, jnp.where(place == 1, label - 256 * high, 0))
    packed_ref[:, width:] = tail.astype(F32).astype(BF)
    txt_hat, txt_inv_ref[...] = normalize(txt_ref[...])
    txt = txt_hat.astype(BF)
    for i in range(copies_ref.shape[0]):
        copies_ref[i] = txt


def project_back(raw, inverse, dnorm):
    hat = raw.astype(F32) * inverse
    return (dnorm - hat * jnp.sum(hat * dnorm, axis=-1, keepdims=True)) * inverse


def pair_products(
    packed_ref, txt_ref, column_ref, scalar_ref,
    mine_ref, before_ref, after_ref, own_part_ref, far_part_ref, grad,
):
    width = txt_ref.shape[1]
    half = own_part_ref.shape[0]
    y = mine_ref.shape[1]
    step = packed_ref.shape[0] // 2
    for start in (0, step):
        rows = slice(start, start + step)
        scores = lax.dot_general(
            packed_ref[rows, :width], txt_ref[...], (((1,), (1,)), ((), ())), preferred_element_type=F32
        )
        mark = packed_ref[rows, width:].astype(F32)
        positive = (mark[:, 0:1] * 256.0 + mark[:, 1:2] == column_ref[...]).astype(F32)
        logits = scalar_ref[0] * scores + scalar_ref[1]
        grad[rows, :] = (jax.nn.sigmoid(logits) - positive).astype(BF)
    part = jnp.dot(grad[...], txt_ref[...], preferred_element_type=F32)
    for i in range(3):
        mine_ref[i] = part[i * y : (i + 1) * y]
    before_ref[...] = part[3 * y : 6 * y].astype(BF)
    after_ref[...] = part[6 * y :].astype(BF)
    for columns, part_ref in ((slice(half, 2 * half), far_part_ref), (slice(0, half), own_part_ref)):
        part_ref[...] = lax.dot_general(
            grad[:, columns],
            packed_ref[:, :width],
            (((0,), (0,)), ((), ())),
            preferred_element_type=F32,
        ).astype(part_ref.dtype)


def exchange(blocks, axes):
    groups = None
    if axes == Z:
        groups = [list(range(i, i + RUN)) for i in range(0, lax.axis_size(Z), RUN)]
    return lax.all_to_all(
        blocks, axes, split_axis=0, concat_axis=0, axis_index_groups=groups, tiled=True
    )


def spread(block, axes, count):
    copies = jnp.broadcast_to(block[None], (count,) + block.shape)
    return joined(exchange(copies, axes))


def joined(blocks):
    return blocks.reshape(-1, blocks.shape[-1])


def scattered(part, axes, count):
    blocks = part.astype(BF).reshape(count, part.shape[0] // count, part.shape[1])
    return exchange(blocks, axes)


def send(x, axis, hop):
    size = lax.axis_size(axis)
    return lax.ppermute(x.astype(BF), axis, [(i, (i + hop) % size) for i in range(size)])


def on_device(img_raw, txt_raw, labels, log_logit_scale, bias):
    blk, width = img_raw.shape
    n_z, n_zl, n_x, n_c, n_y = (lax.axis_size(a) for a in (Z, "zl", "x", "c", "y"))
    temperature = jnp.exp(log_logit_scale[0])
    shift = bias[0]
    vmem = pl.BlockSpec(memory_space=pltpu.VMEM)
    packed, txt, img_inv, txt_inv = pl.pallas_call(
        prepare,
        out_shape=[
            jax.ShapeDtypeStruct((blk, width + 128), BF),
            jax.ShapeDtypeStruct((RUN, blk, width), BF),
            jax.ShapeDtypeStruct((blk, 1), F32),
            jax.ShapeDtypeStruct((blk, 1), F32),
        ],
        in_specs=[vmem] * 3,
        out_specs=[vmem] * 4,
    )(img_raw, txt_raw, labels.reshape(1, blk))

    trio = jnp.concatenate([packed, send(packed, Z, -RUN), send(packed, Z, RUN)])
    trio, txt = lax.optimization_barrier((trio, joined(exchange(txt, Z))))
    wide = jnp.concatenate([send(trio, "y", 3), trio, send(trio, "y", -3)])
    y = trio.shape[0]
    packed = jnp.concatenate([wide, send(wide, "y", -1), send(wide[y:], "y", 1)])
    txt = spread(txt, "x", n_x)
    half = txt.shape[0]
    packed, txt = lax.optimization_barrier((packed, txt))
    txt = jnp.concatenate([txt, send(txt, "c", 1)])

    owner = jnp.arange(n_c * n_x * RUN, dtype=jnp.int32)
    at_z = lax.axis_index(Z) // RUN * RUN + owner % RUN
    at_x = owner // RUN % n_x
    at_c = (lax.axis_index("c") + owner // (RUN * n_x)) % n_c
    col = at_z % n_zl * n_y + lax.axis_index("y")
    block = ((col * (n_z // n_zl) + at_z // n_zl) * n_x + at_x) * n_c + at_c
    columns = block[:, None] * blk + jnp.arange(blk, dtype=jnp.int32)[None, :]
    mine, away, back, own_part, far_part = pl.pallas_call(
        pair_products,
        out_shape=[
            jax.ShapeDtypeStruct((3, y, width), F32),
            jax.ShapeDtypeStruct((3 * y, width), BF),
            jax.ShapeDtypeStruct((2 * y, width), BF),
            jax.ShapeDtypeStruct((half, width), F32),
            jax.ShapeDtypeStruct((half, width), BF),
        ],
        in_specs=[vmem] * 3 + [pl.BlockSpec(memory_space=pltpu.SMEM)],
        out_specs=[vmem] * 5,
        scratch_shapes=[pltpu.VMEM((packed.shape[0], 2 * half), BF)],
        compiler_params=pltpu.CompilerParams(vmem_limit_bytes=24 * 1024 * 1024),
    )(packed, txt, columns.reshape(1, -1).astype(F32), jnp.stack([temperature, shift]))
    before, after = send(away, "y", 1), send(back, "y", -1)
    txt_sum = own_part + send(far_part, "c", 1).astype(F32)
    txt_sum = jnp.sum(scattered(txt_sum, "x", n_x).astype(F32), axis=0)
    txt_sum = jnp.sum(scattered(txt_sum, Z, RUN).astype(F32), axis=0)

    low = mine[0] + before[:y].astype(F32)
    mid = mine[1] + before[y : 2 * y].astype(F32) + after[:y].astype(F32)
    top = mine[2] + before[2 * y :].astype(F32) + after[y:].astype(F32)
    mid = mid + send(low, "y", -3).astype(F32) + send(top, "y", 3).astype(F32)
    one, two = send(mid[blk : 2 * blk], Z, RUN), send(mid[2 * blk :], Z, -RUN)
    img_sum = mid[:blk] + one.astype(F32) + two.astype(F32)
    return (
        project_back(img_raw, img_inv, temperature * img_sum),
        project_back(txt_raw, txt_inv, temperature * txt_sum),
    )


def solution(mesh):
    fine = Mesh(mesh.devices.reshape(4, 4, 2, 3, 8), ("zh", "x", "c", "zl", "y"))
    row, col = ("zh", "x", "c"), ("zl", "y")
    return jax.shard_map(
        on_device,
        mesh=fine,
        in_specs=(P(row + col, None), P(col + row, None), P(row + col), P(), P()),
        out_specs=(P(row + col, None), P(col + row, None)),
        check_vma=False,
    )
```

```python
import jax
import jax.numpy as jnp
from jax import lax
from jax.experimental import pallas as pl
from jax.experimental.pallas import tpu as pltpu
from jax.sharding import Mesh, PartitionSpec as P

EPS = 1e-06
BF = jnp.bfloat16
F32 = jnp.float32
Z = ("zh", "zl")
RUN = 4


def normalize(raw):
    wide = raw.astype(F32)
    inverse = lax.rsqrt(jnp.sum(wide * wide, axis=-1, keepdims=True) + EPS)
    return (wide * inverse, inverse)


def prepare(img_ref, txt_ref, label_ref, packed_ref, copies_ref, img_inv_ref, txt_inv_ref):
    blk, width = img_ref.shape
    img_hat, img_inv_ref[...] = normalize(img_ref[...])
    packed_ref[:, :width] = img_hat.astype(BF)
    row = lax.broadcasted_iota(jnp.int32, (blk, blk), 0)
    lane = lax.broadcasted_iota(jnp.int32, (blk, blk), 1)
    spot = jnp.where(row == lane, label_ref[...].astype(F32), 0.0)
    label = jnp.sum(spot, axis=1, keepdims=True).astype(jnp.int32)
    high = label >> 8
    place = lax.broadcasted_iota(jnp.int32, (blk, packed_ref.shape[1] - width), 1)
    tail = jnp.where(place == 0, high, jnp.where(place == 1, label - 256 * high, 0))
    packed_ref[:, width:] = tail.astype(F32).astype(BF)
    txt_hat, txt_inv_ref[...] = normalize(txt_ref[...])
    txt = txt_hat.astype(BF)
    for i in range(copies_ref.shape[0]):
        copies_ref[i] = txt


def project_back(raw, inverse, dnorm):
    hat = raw.astype(F32) * inverse
    return (dnorm - hat * jnp.sum(hat * dnorm, axis=-1, keepdims=True)) * inverse


def exchange(blocks, axes):
    groups = None
    if axes == Z:
        groups = [list(range(i, i + RUN)) for i in range(0, lax.axis_size(Z), RUN)]
    return lax.all_to_all(
        blocks, axes, split_axis=0, concat_axis=0, axis_index_groups=groups, tiled=True
    )


def spread(block, axes, count):
    copies = jnp.broadcast_to(block[None], (count,) + block.shape)
    return joined(exchange(copies, axes))


def joined(blocks):
    return blocks.reshape(-1, blocks.shape[-1])


def scattered(part, axes, count):
    blocks = part.astype(BF).reshape(count, part.shape[0] // count, part.shape[1])
    return exchange(blocks, axes)


def send(x, axis, hop):
    size = lax.axis_size(axis)
    return lax.ppermute(x.astype(BF), axis, [(i, (i + hop) % size) for i in range(size)])


def on_device(img_raw, txt_raw, labels, log_logit_scale, bias):
    blk, width = img_raw.shape
    n_z, n_zl, n_x, n_c, n_y = (lax.axis_size(a) for a in (Z, "zl", "x", "c", "y"))
    temperature = jnp.exp(log_logit_scale[0])
    shift = bias[0]
    vmem = pl.BlockSpec(memory_space=pltpu.VMEM)
    packed, txt, img_inv, txt_inv = pl.pallas_call(
        prepare,
        out_shape=[
            jax.ShapeDtypeStruct((blk, width + 128), BF),
            jax.ShapeDtypeStruct((RUN, blk, width), BF),
            jax.ShapeDtypeStruct((blk, 1), F32),
            jax.ShapeDtypeStruct((blk, 1), F32),
        ],
        in_specs=[vmem] * 3,
        out_specs=[vmem] * 4,
    )(img_raw, txt_raw, labels.reshape(1, blk))

    trio = jnp.concatenate([packed, send(packed, Z, -RUN), send(packed, Z, RUN)])
    trio, txt = lax.optimization_barrier((trio, joined(exchange(txt, Z))))
    wide = jnp.concatenate([send(trio, "y", 3), trio, send(trio, "y", -3)])
    y = trio.shape[0]
    part = y // 16 * 8 + 8
    packed = jnp.concatenate([wide, send(wide[: 2 * y + part], "y", -1), send(wide[part:], "y", 1)])
    txt = spread(txt, "x", n_x)
    half = txt.shape[0]
    txt = jnp.concatenate([txt, send(txt, "c", 1)])

    img = packed[:, :width]
    marks = packed[:, width : width + 2].astype(F32)
    target = (marks[:, :1] * 256.0 + marks[:, 1:]).astype(jnp.int32)

    owner = jnp.arange(n_c * n_x * RUN, dtype=jnp.int32)
    at_z = lax.axis_index(Z) // RUN * RUN + owner % RUN
    at_x = owner // RUN % n_x
    at_c = (lax.axis_index("c") + owner // (RUN * n_x)) % n_c
    col = at_z % n_zl * n_y + lax.axis_index("y")
    block = ((col * (n_z // n_zl) + at_z // n_zl) * n_x + at_x) * n_c + at_c
    columns = block[:, None] * blk + jnp.arange(blk, dtype=jnp.int32)[None, :]
    scores = lax.dot_general(img, txt, (((1,), (1,)), ((), ())), preferred_element_type=F32)
    positive = (target == columns.reshape(1, -1)).astype(F32)
    grad = (jax.nn.sigmoid(temperature * scores + shift) - positive).astype(BF)

    def txt_part(block):
        return lax.dot_general(block, img, (((0,), (0,)), ((), ())), preferred_element_type=F32)

    away = jnp.dot(grad[3 * y :], txt, preferred_element_type=F32).astype(BF)
    away, grad = lax.optimization_barrier((away, grad))
    before, after = send(away[: 2 * y + part], "y", 1), send(away[2 * y + part :], "y", -1)

    arrived = send(txt_part(grad[:, half:]), "c", 1)
    txt_sum = txt_part(grad[:, :half]) + arrived.astype(F32)
    txt_sum = jnp.sum(scattered(txt_sum, "x", n_x).astype(F32), axis=0)
    txt_sum = jnp.sum(scattered(txt_sum, Z, RUN).astype(F32), axis=0)

    mine = jnp.dot(grad[: 3 * y], txt, preferred_element_type=F32)
    rest = y - part
    before, after = before.astype(F32), after.astype(F32)
    low = mine[:y] + before[:y] + jnp.pad(after[:rest], ((part, 0), (0, 0)))
    mid = mine[y : 2 * y] + before[y : 2 * y] + after[rest : rest + y]
    top = mine[2 * y :] + jnp.pad(before[2 * y :], ((0, rest), (0, 0))) + after[rest + y :]
    mid = mid + send(low, "y", -3).astype(F32) + send(top, "y", 3).astype(F32)
    one, two = send(mid[blk : 2 * blk], Z, RUN), send(mid[2 * blk :], Z, -RUN)
    img_sum = mid[:blk] + one.astype(F32) + two.astype(F32)
    return (
        project_back(img_raw, img_inv, temperature * img_sum),
        project_back(txt_raw, txt_inv, temperature * txt_sum),
    )


def solution(mesh):
    fine = Mesh(mesh.devices.reshape(4, 4, 2, 3, 8), ("zh", "x", "c", "zl", "y"))
    row, col = ("zh", "x", "c"), ("zl", "y")
    return jax.shard_map(
        on_device,
        mesh=fine,
        in_specs=(P(row + col, None), P(col + row, None), P(row + col), P(), P()),
        out_specs=(P(row + col, None), P(col + row, None)),
        check_vma=False,
    )
```

```python
import jax
import jax.numpy as jnp
from jax import lax
from jax.experimental import pallas as pl
from jax.experimental.pallas import tpu as pltpu
from jax.sharding import Mesh, PartitionSpec as P

EPS = 1e-06
BF = jnp.bfloat16
F32 = jnp.float32
Z = ("zh", "zl")
RUN = 4


def normalize(raw):
    wide = raw.astype(F32)
    inverse = lax.rsqrt(jnp.sum(wide * wide, axis=-1, keepdims=True) + EPS)
    return (wide * inverse, inverse)


def prepare(img_ref, txt_ref, label_ref, packed_ref, copies_ref, img_inv_ref, txt_inv_ref):
    blk, width = img_ref.shape
    img_hat, img_inv_ref[...] = normalize(img_ref[...])
    packed_ref[:, :width] = img_hat.astype(BF)
    row = lax.broadcasted_iota(jnp.int32, (blk, blk), 0)
    lane = lax.broadcasted_iota(jnp.int32, (blk, blk), 1)
    spot = jnp.where(row == lane, label_ref[...].astype(F32), 0.0)
    label = jnp.sum(spot, axis=1, keepdims=True).astype(jnp.int32)
    high = label >> 8
    place = lax.broadcasted_iota(jnp.int32, (blk, packed_ref.shape[1] - width), 1)
    tail = jnp.where(place == 0, high, jnp.where(place == 1, label - 256 * high, 0))
    packed_ref[:, width:] = tail.astype(F32).astype(BF)
    txt_hat, txt_inv_ref[...] = normalize(txt_ref[...])
    txt = txt_hat.astype(BF)
    for i in range(copies_ref.shape[0]):
        copies_ref[i] = txt


def project_back(raw, inverse, dnorm):
    hat = raw.astype(F32) * inverse
    return (dnorm - hat * jnp.sum(hat * dnorm, axis=-1, keepdims=True)) * inverse


def exchange(blocks, axes):
    groups = None
    if axes == Z:
        groups = [list(range(i, i + RUN)) for i in range(0, lax.axis_size(Z), RUN)]
    return lax.all_to_all(
        blocks, axes, split_axis=0, concat_axis=0, axis_index_groups=groups, tiled=True
    )


def spread(block, axes, count):
    copies = jnp.broadcast_to(block[None], (count,) + block.shape)
    return joined(exchange(copies, axes))


def joined(blocks):
    return blocks.reshape(-1, blocks.shape[-1])


def scattered(part, axes, count):
    blocks = part.astype(BF).reshape(count, part.shape[0] // count, part.shape[1])
    return exchange(blocks, axes)


def send(x, axis, hop):
    size = lax.axis_size(axis)
    return lax.ppermute(x.astype(BF), axis, [(i, (i + hop) % size) for i in range(size)])


def on_device(img_raw, txt_raw, labels, log_logit_scale, bias):
    blk, width = img_raw.shape
    n_z, n_zl, n_x, n_c, n_y = (lax.axis_size(a) for a in (Z, "zl", "x", "c", "y"))
    temperature = jnp.exp(log_logit_scale[0])
    shift = bias[0]
    vmem = pl.BlockSpec(memory_space=pltpu.VMEM)
    packed, txt, img_inv, txt_inv = pl.pallas_call(
        prepare,
        out_shape=[
            jax.ShapeDtypeStruct((blk, width + 128), BF),
            jax.ShapeDtypeStruct((RUN, blk, width), BF),
            jax.ShapeDtypeStruct((blk, 1), F32),
            jax.ShapeDtypeStruct((blk, 1), F32),
        ],
        in_specs=[vmem] * 3,
        out_specs=[vmem] * 4,
    )(img_raw, txt_raw, labels.reshape(1, blk))

    trio = jnp.concatenate([packed, send(packed, Z, -RUN), send(packed, Z, RUN)])
    trio, txt = lax.optimization_barrier((trio, joined(exchange(txt, Z))))
    wide = jnp.concatenate([send(trio, "y", 3), trio, send(trio, "y", -3)])
    y = trio.shape[0]
    part = y // 16 * 8 + 8
    packed = jnp.concatenate([wide, send(wide[: 2 * y + part], "y", -1), send(wide[part:], "y", 1)])
    txt = spread(txt, "x", n_x)
    half = txt.shape[0]
    txt = jnp.concatenate([txt, send(txt, "c", 1)])

    img = packed[:, :width]
    marks = packed[:, width : width + 2].astype(F32)
    target = (marks[:, :1] * 256.0 + marks[:, 1:]).astype(jnp.int32)

    owner = jnp.arange(n_c * n_x * RUN, dtype=jnp.int32)
    at_z = lax.axis_index(Z) // RUN * RUN + owner % RUN
    at_x = owner // RUN % n_x
    at_c = (lax.axis_index("c") + owner // (RUN * n_x)) % n_c
    col = at_z % n_zl * n_y + lax.axis_index("y")
    block = ((col * (n_z // n_zl) + at_z // n_zl) * n_x + at_x) * n_c + at_c
    columns = block[:, None] * blk + jnp.arange(blk, dtype=jnp.int32)[None, :]
    scores = lax.dot_general(img, txt, (((1,), (1,)), ((), ())), preferred_element_type=F32)
    positive = (target == columns.reshape(1, -1)).astype(F32)
    grad = (jax.nn.sigmoid(temperature * scores + shift) - positive).astype(BF)

    def txt_part(block):
        return lax.dot_general(block, img, (((0,), (0,)), ((), ())), preferred_element_type=F32)

    away = jnp.dot(grad[3 * y :], txt, preferred_element_type=F32).astype(BF)
    away, grad = lax.optimization_barrier((away, grad))
    before, after = send(away[: 2 * y + part], "y", 1), send(away[2 * y + part :], "y", -1)

    arrived = send(txt_part(grad[:, half:]), "c", 1)
    txt_sum = txt_part(grad[:, :half]) + arrived.astype(F32)
    txt_sum = jnp.sum(scattered(txt_sum, "x", n_x).astype(F32), axis=0)
    txt_sum = jnp.sum(scattered(txt_sum, Z, RUN).astype(F32), axis=0)

    mine = jnp.dot(grad[: 3 * y], txt, preferred_element_type=F32)
    rest = y - part
    before, after = before.astype(F32), after.astype(F32)
    low = mine[:y] + before[:y] + jnp.pad(after[:rest], ((part, 0), (0, 0)))
    mid = mine[y : 2 * y] + before[y : 2 * y] + after[rest : rest + y]
    top = mine[2 * y :] + jnp.pad(before[2 * y :], ((0, rest), (0, 0))) + after[rest + y :]
    mid = mid + send(low, "y", -3).astype(F32) + send(top, "y", 3).astype(F32)
    mid, txt_sum = lax.optimization_barrier((mid, txt_sum))
    one, two = send(mid[blk : 2 * blk], Z, RUN), send(mid[2 * blk :], Z, -RUN)
    img_sum = mid[:blk] + one.astype(F32) + two.astype(F32)
    return (
        project_back(img_raw, img_inv, temperature * img_sum),
        project_back(txt_raw, txt_inv, temperature * txt_sum),
    )


def solution(mesh):
    fine = Mesh(mesh.devices.reshape(4, 4, 2, 3, 8), ("zh", "x", "c", "zl", "y"))
    row, col = ("zh", "x", "c"), ("zl", "y")
    return jax.shard_map(
        on_device,
        mesh=fine,
        in_specs=(P(row + col, None), P(col + row, None), P(row + col), P(), P()),
        out_specs=(P(row + col, None), P(col + row, None)),
        check_vma=False,
    )
```
